32 devices in a mesh: grp: 2 (over y), seq: 4 (over z), head: 2 (over x), sub: 2 (over core).
Axes of the slice: x: 2, y: 2, z: 4, core: 2. Of those that a mesh axis runs over, the one named last changes fastest.
Arguments:
- queries: bfloat16 [4096, 64, 128], P(('grp', 'seq', 'sub'), 'head'), parts along dimension 0, may hold values from -240 to 240
- keys: bfloat16 [4096, 8, 128], P(('grp', 'seq', 'sub'), 'head'), parts along dimension 0, may hold values from -240 to 240
- values: bfloat16 [4096, 8, 128], P(('grp', 'seq', 'sub'), 'head'), parts along dimension 0, may hold values from -6 to 6
- out_grad: bfloat16 [4096, 64, 128], P(('grp', 'seq', 'sub'), 'head'), parts along dimension 0, may hold values from -48 to 48
- feature_weights: bfloat16 [2, 64, 128, 128], P(None, 'head'), may hold values from -1.5 to 1.5
Outputs:
- query_grad: bfloat16 [4096, 64, 128], P(('grp', 'seq', 'sub'), 'head'), parts along dimension 0
- key_grad: bfloat16 [4096, 8, 128], P(('grp', 'seq', 'sub'), 'head'), parts along dimension 0
- value_grad: bfloat16 [4096, 8, 128], P(('grp', 'seq', 'sub'), 'head'), parts along dimension 0
- map_grads: float32 [256, 2, 64, 128], P(('grp', 'seq', 'sub'), None, 'head'), parts along dimension 0
The draws below stay inside these ranges and needn't reach their ends.
There are 2 independent parts, one for each index of `grp`. The reference program is written for one: setup_inputs(seed, part) draws one part's arguments, and reference() takes and returns one part's arrays. A program takes and returns all parts, laid end to end along the dimension named above; an argument that names none is the same for every part. Nothing has to cross between parts.
All inputs are finite; a program needn't handle non-finite values.
Results may differ from the reference program's by a relative error of at most 0.014.
Values sent between devices are 32-bit elements; how exact they have to be, the bound alone decides.
A program may use at most 192 MiB of HBM per device.

```python
import jax
import jax.numpy as jnp
from jax import lax

QH = 64
KVH = 8
HD = 128
FEAT = 128
TOK_DEV = 256
SEQLEN = 2048


def boosted_rows(key, heads, chance):
    base_key, pick_key, size_key = jax.random.split(key, 3)
    base = jnp.clip(jax.random.normal(base_key, (SEQLEN, heads, HD), jnp.float32), -6.0, 6.0)
    position = jnp.arange(SEQLEN)[:, None, None]
    picked = (jax.random.uniform(pick_key, (SEQLEN, 1, 1)) < chance) & (position >= 64)
    strength = jax.random.uniform(size_key, (SEQLEN, 1, 1), minval=0.6, maxval=1.0)
    return jnp.where(picked, base * strength, base)


def draw_queries(key, part):
    key = jax.random.fold_in(key, 11)
    chance = 0.0
    return boosted_rows(key, QH, chance).astype(jnp.bfloat16)


def draw_keys(key, part):
    key = jax.random.fold_in(key, 23)
    chance = 0.0
    return boosted_rows(key, KVH, chance).astype(jnp.bfloat16)


def levels(key, extent, cuts, low, largest):
    factor_of = 1.0
    for dim, blocks in cuts:
        draws = jax.random.uniform(jax.random.fold_in(jax.random.fold_in(key, 6), dim), (blocks,), jnp.float32, low / len(cuts), largest / len(cuts))
        factor_of = factor_of * jnp.repeat(jnp.exp(draws), extent[dim] // blocks).reshape((-1,) + (1,) * (len(extent) - 1 - dim))
    return factor_of


def noise(own_key, shape, spread, limit, cuts=(), held_as=jnp.bfloat16):
    entries = spread * jax.random.normal(own_key, shape, jnp.float32)
    if cuts:
        entries = entries * levels(own_key, shape, cuts, -0.22, 0.18)
    return jnp.clip(entries, -limit, limit).astype(held_as)


def setup_inputs(seed: int = 0, part: int = 0) -> dict:
    key_of = jax.random.split(jax.random.key(seed), 6)
    part_keys = jax.random.split(jax.random.fold_in(key_of[5], part), 6)
    return {
        "queries": draw_queries(jax.random.fold_in(jax.random.fold_in(key_of[5], part), 71), part),
        "keys": draw_keys(jax.random.fold_in(jax.random.fold_in(key_of[5], part), 71), part),
        "values": noise(part_keys[2], (SEQLEN, KVH, HD), 1.0, 6.0, ((0, 8), (1, 2))),
        "out_grad": noise(part_keys[3], (SEQLEN, QH, HD), 8.0, 48.0, ((0, 8), (1, 2))),
        "feature_weights": noise(key_of[4], (2, QH, HD, FEAT), 0.25, 1.5, ((1, 2),)),
    }


def prod(form, left, right):
    return jnp.einsum(form, left.astype(jnp.float32), right.astype(jnp.float32), precision=lax.Precision.HIGHEST)

def exclusive_sum(stack, reverse):
    if reverse:
        stack = jnp.flip(stack, 0)
    running = jnp.cumsum(stack, axis=0)
    shifted = jnp.concatenate([jnp.zeros_like(stack[:1]), running[:-1]], axis=0)
    if reverse:
        shifted = jnp.flip(shifted, 0)
    return shifted

def feature_map(inputs, weight):
    return jax.nn.softmax(prod('thd,hdf->thf', inputs, weight), axis=-1)

def first_section(block_queries, key_rows, value_rows, query_map, key_map):
    query_feat = feature_map(block_queries, query_map)
    key_feat = feature_map(key_rows, key_map)
    query_low = query_feat.astype(jnp.bfloat16)
    key_low = key_feat.astype(jnp.bfloat16)
    kv_block = prod('thf,thd->hfd', key_low, value_rows)
    z_block = lax.optimization_barrier(jnp.sum(key_low.astype(jnp.float32), axis=0))
    return (query_feat, key_feat, query_low, key_low, kv_block, z_block)

def second_section(query_low, key_low, value_rows, block_grad, state_kv, state_z):
    tokens = query_low.shape[0]
    causal = jnp.arange(tokens)[:, None] >= jnp.arange(tokens)[None, :]
    masked = jnp.where(causal[None], prod('thf,shf->hts', query_low, key_low), 0.0)
    weights = masked.astype(jnp.bfloat16)
    numerator = prod('hts,shd->thd', weights, value_rows) + prod('thf,hfd->thd', query_low, state_kv)
    denominator = lax.optimization_barrier(jnp.sum(masked, axis=2)).T + prod('thf,hf->th', query_low, state_z)
    grad_wide = block_grad.astype(jnp.float32)
    numer_grad = (grad_wide / denominator[:, :, None]).astype(jnp.bfloat16)
    denom_grad = -lax.optimization_barrier(jnp.sum(grad_wide * numerator, axis=2)) / (denominator * denominator)
    back_block = prod('thf,thd->hfd', query_low, numer_grad)
    back_z_block = prod('th,thf->hf', denom_grad, query_low)
    return (causal, weights, numer_grad, denom_grad, back_block, back_z_block)

def logit_grad(feat, grad):
    return (feat * (grad - lax.optimization_barrier(jnp.sum(feat * grad, axis=-1, keepdims=True)))).astype(jnp.bfloat16)

def group_backward(pieces):
    group_queries, group_keys, group_values, group_grad, maps = pieces
    group_size = group_queries.shape[1]
    block_count = SEQLEN // TOK_DEV
    query_blocks = group_queries.reshape(block_count, TOK_DEV, group_size, HD)
    grad_blocks = group_grad.reshape(block_count, TOK_DEV, group_size, HD)
    key_rows = jnp.broadcast_to(group_keys.reshape(block_count, TOK_DEV, 1, HD), (block_count, TOK_DEV, group_size, HD))
    value_rows = jnp.broadcast_to(group_values.reshape(block_count, TOK_DEV, 1, HD), (block_count, TOK_DEV, group_size, HD))

    def section_one(item):
        return first_section(item[0], item[1], item[2], maps[0], maps[1])[4:]
    kv_blocks, z_blocks = lax.map(section_one, (query_blocks, key_rows, value_rows))
    state_kv = exclusive_sum(kv_blocks, False)
    state_z = exclusive_sum(z_blocks, False)

    def section_two(item):
        first = first_section(item[0], item[1], item[2], maps[0], maps[1])
        return second_section(first[2], first[3], item[2], item[3], item[4], item[5])[4:]
    back_blocks, back_z_blocks = lax.map(section_two, (query_blocks, key_rows, value_rows, grad_blocks, state_kv, state_z))
    back_state = exclusive_sum(back_blocks, True)
    back_z = exclusive_sum(back_z_blocks, True)

    def section_three(item):
        block_queries, block_keys, block_values, block_grad, one_kv, one_z, one_back, one_back_z = item
        query_feat, key_feat, query_low, key_low, kv_unused, z_unused = first_section(block_queries, block_keys, block_values, maps[0], maps[1])
        causal, weights, numer_grad, denom_grad, back_unused, back_z_unused = second_section(query_low, key_low, block_values, block_grad, one_kv, one_z)
        score_grad = jnp.where(causal[None], prod('thd,shd->hts', numer_grad, block_values) + denom_grad.T[:, :, None], 0.0).astype(jnp.bfloat16)
        query_feat_grad = prod('hts,shf->thf', score_grad, key_low) + prod('thd,hfd->thf', numer_grad, one_kv) + denom_grad[:, :, None] * one_z[None]
        key_feat_grad = prod('hts,thf->shf', score_grad, query_low) + prod('shd,hfd->shf', block_values, one_back) + one_back_z[None]
        value_sum = prod('hts,thd->shd', weights, numer_grad) + prod('shf,hfd->shd', key_low, one_back)
        query_logit_grad = logit_grad(query_feat, query_feat_grad)
        key_logit_grad = logit_grad(key_feat, key_feat_grad)
        query_grad = prod('thf,hdf->thd', query_logit_grad, maps[0]).astype(jnp.bfloat16)
        key_grad = lax.optimization_barrier(jnp.sum(prod('thf,hdf->thd', key_logit_grad, maps[1]), axis=1)).astype(jnp.bfloat16)
        value_grad = lax.optimization_barrier(jnp.sum(value_sum, axis=1)).astype(jnp.bfloat16)
        map_term = jnp.stack([prod('thd,thf->dhf', block_queries, query_logit_grad), prod('thd,thf->dhf', block_keys, key_logit_grad)], axis=1)
        return (query_grad, key_grad, value_grad, map_term)
    outputs = lax.map(section_three, (query_blocks, key_rows, value_rows, grad_blocks, state_kv, state_z, back_state, back_z))
    return (outputs[0].reshape(SEQLEN, group_size, HD), outputs[1].reshape(SEQLEN, HD), outputs[2].reshape(SEQLEN, HD), lax.optimization_barrier(jnp.sum(outputs[3], axis=0)))

def reference(queries, keys, values, out_grad, feature_weights):
    group_size = QH // KVH
    grouped_queries = queries.reshape(SEQLEN, KVH, group_size, HD).transpose(1, 0, 2, 3)
    grouped_grad = out_grad.reshape(SEQLEN, KVH, group_size, HD).transpose(1, 0, 2, 3)
    grouped_keys = keys.transpose(1, 0, 2)
    grouped_values = values.transpose(1, 0, 2)
    grouped_maps = feature_weights.reshape(2, KVH, group_size, HD, FEAT).transpose(1, 0, 2, 3, 4)
    query_grad, key_grad, value_grad, map_grads = lax.map(group_backward, (grouped_queries, grouped_keys, grouped_values, grouped_grad, grouped_maps))
    query_grad = query_grad.transpose(1, 0, 2, 3).reshape(SEQLEN, QH, HD)
    key_grad = key_grad.transpose(1, 0, 2)
    value_grad = value_grad.transpose(1, 0, 2)
    map_grads = map_grads.transpose(1, 2, 0, 3, 4).reshape(HD, 2, QH, FEAT)
    return (query_grad, key_grad, value_grad, map_grads)
```

```python
import functools

import jax
import jax.numpy as jnp
from jax import lax
from jax.experimental import pallas as pl
from jax.experimental.pallas import tpu as pltpu
from jax.sharding import PartitionSpec as P

F32 = jnp.float32
BF16 = jnp.bfloat16


def dot(left, right, left_dim, right_dim):
    return lax.dot_general(
        left, right, (((left_dim,), (right_dim,)), ((), ())), preferred_element_type=F32
    )


def softmax(logits):
    grown = jnp.exp(logits - jnp.max(logits, axis=1, keepdims=True))
    return grown * (1.0 / jnp.sum(grown, axis=1, keepdims=True))


def logit_grad(low, grad):
    feat = low.astype(F32)
    return (feat * (grad - jnp.sum(feat * grad, axis=1, keepdims=True))).astype(BF16)


def kernel(
    blocks, subs, group_size,
    q_ref, k_ref, v_ref, og_ref, w_ref,
    qg_ref, kg_ref, vg_ref, mg_ref,
    ql_ref, kl_ref, ng_ref, dg_ref, wt_ref,
    fwd_in, fwd_out, bwd_in, bwd_out, k_acc, v_acc,
    fwd_send, fwd_recv, bwd_send, bwd_recv,
):
    heads, tokens, width = q_ref.shape
    feats = w_ref.shape[3]
    me = lax.axis_index("seq") * subs + lax.axis_index("sub")
    first = me == 0
    last = me == blocks - 1
    before = jnp.maximum(me - 1, 0)
    after = jnp.minimum(me + 1, blocks - 1)

    def place(block):
        return {"seq": block // subs, "sub": block % subs}

    def fwd_copy(h):
        return pltpu.make_async_remote_copy(
            src_ref=fwd_out.at[h], dst_ref=fwd_in.at[h],
            send_sem=fwd_send.at[h], recv_sem=fwd_recv.at[h],
            device_id=place(after), device_id_type=pl.DeviceIdType.MESH,
        )

    def bwd_copy(h):
        return pltpu.make_async_remote_copy(
            src_ref=bwd_out.at[h], dst_ref=bwd_in.at[h],
            send_sem=bwd_send.at[h], recv_sem=bwd_recv.at[h],
            device_id=place(before), device_id_type=pl.DeviceIdType.MESH,
        )

    barrier = pltpu.get_barrier_semaphore()

    @pl.when(me > 0)
    def _():
        pl.semaphore_signal(
            barrier, inc=1, device_id=place(before), device_id_type=pl.DeviceIdType.MESH
        )

    @pl.when(me < blocks - 1)
    def _():
        pl.semaphore_signal(
            barrier, inc=1, device_id=place(after), device_id_type=pl.DeviceIdType.MESH
        )

    inner = jnp.logical_and(me > 0, me < blocks - 1)

    @pl.when(inner)
    def _():
        pl.semaphore_wait(barrier, 2)

    @pl.when(jnp.logical_not(inner))
    def _():
        pl.semaphore_wait(barrier, 1)

    @pl.when(first)
    def _():
        fwd_in[...] = jnp.zeros_like(fwd_in)

    @pl.when(last)
    def _():
        bwd_in[...] = jnp.zeros_like(bwd_in)

    def features(h, carry):
        g = h // group_size
        ql_ref[h] = softmax(dot(q_ref[h], w_ref[0, h], 1, 0)).astype(BF16)
        key_low = softmax(dot(k_ref[g], w_ref[1, h], 1, 0)).astype(BF16)
        kl_ref[h] = key_low
        own = dot(v_ref[g], key_low, 0, 0)
        own_z = jnp.sum(key_low.astype(F32), axis=0, keepdims=True)

        @pl.when(me > 0)
        def _():
            fwd_copy(h).wait_recv()

        @pl.when(me < blocks - 1)
        def _():
            fwd_out[h, 0:width] = fwd_in[h, 0:width] + own
            fwd_out[h, width:width + 8] = fwd_in[h, width:width + 8] + own_z
            fwd_copy(h).start()

        return carry

    lax.fori_loop(0, heads, features, 0)

    def causal():
        rows = lax.broadcasted_iota(jnp.int32, (tokens, tokens), 0)
        return rows >= lax.broadcasted_iota(jnp.int32, (tokens, tokens), 1)

    def forward(h, carry):
        g = h // group_size
        query_low = ql_ref[h]
        masked = jnp.where(causal(), dot(query_low, kl_ref[h], 1, 1), 0.0)
        weights = masked.astype(BF16)
        wt_ref[h] = weights
        numerator = dot(weights, v_ref[g], 1, 0) + dot(
            query_low, fwd_in[h, 0:width].astype(BF16), 1, 1
        )
        query_round = query_low.astype(F32)
        denominator = jnp.sum(masked, axis=1, keepdims=True) + jnp.sum(
            query_round * fwd_in[h, width:width + 1], axis=1, keepdims=True
        )
        grad = og_ref[h].astype(F32)
        numer_grad = (grad * (1.0 / denominator)).astype(BF16)
        denom_grad = -jnp.sum(grad * numerator, axis=1, keepdims=True) / (
            denominator * denominator
        )
        ng_ref[h] = numer_grad
        dg_ref[h] = denom_grad
        own = dot(numer_grad, query_low, 0, 0)
        own_z = jnp.sum(query_round * denom_grad, axis=0, keepdims=True)

        @pl.when(me < blocks - 1)
        def _():
            bwd_copy(h).wait_recv()

        @pl.when(me > 0)
        def _():
            bwd_out[h, 0:width] = bwd_in[h, 0:width] + own
            bwd_out[h, width:width + 8] = bwd_in[h, width:width + 8] + own_z
            bwd_copy(h).start()

        return carry

    lax.fori_loop(0, heads, forward, 0)

    def backward(h, carry):
        g = h // group_size
        query_low = ql_ref[h]
        key_low = kl_ref[h]
        numer_grad = ng_ref[h]
        denom_grad = dg_ref[h]
        value_rows = v_ref[g]
        score_grad = jnp.where(
            causal(), dot(numer_grad, value_rows, 1, 1) + denom_grad, 0.0
        ).astype(BF16)
        query_feat_grad = (
            dot(score_grad, key_low, 1, 0)
            + dot(numer_grad, fwd_in[h, 0:width].astype(BF16), 1, 0)
            + denom_grad * fwd_in[h, width:width + 1]
        )
        query_logit_grad = logit_grad(query_low, query_feat_grad)
        qg_ref[h] = dot(query_logit_grad, w_ref[0, h], 1, 1).astype(BF16)
        parts = mg_ref.shape[0]
        mg_ref[:, 0, h] = dot(q_ref[h], query_logit_grad, 0, 0).reshape(
            parts, width // parts, feats
        )
        back = bwd_in[h, 0:width].astype(BF16)
        key_feat_grad = (
            dot(score_grad, query_low, 0, 0)
            + dot(value_rows, back, 1, 0)
            + bwd_in[h, width:width + 1]
        )
        key_logit_grad = logit_grad(key_low, key_feat_grad)
        mg_ref[:, 1, h] = dot(k_ref[g], key_logit_grad, 0, 0).reshape(
            parts, width // parts, feats
        )
        key_term = dot(key_logit_grad, w_ref[1, h], 1, 1)
        value_term = dot(wt_ref[h], numer_grad, 0, 0) + dot(key_low, back, 1, 1)
        fresh = h % group_size == 0

        @pl.when(fresh)
        def _():
            k_acc[...] = key_term
            v_acc[...] = value_term

        @pl.when(jnp.logical_not(fresh))
        def _():
            k_acc[...] += key_term
            v_acc[...] += value_term

        @pl.when(h % group_size == group_size - 1)
        def _():
            kg_ref[g] = k_acc[...].astype(BF16)
            vg_ref[g] = v_acc[...].astype(BF16)

        return carry

    lax.fori_loop(0, heads, backward, 0)

    def drain(h, carry):
        @pl.when(me < blocks - 1)
        def _():
            fwd_copy(h).wait_send()

        @pl.when(me > 0)
        def _():
            bwd_copy(h).wait_send()

        return carry

    lax.fori_loop(0, heads, drain, 0)


def shards(blocks, subs, queries, keys, values, out_grad, feature_weights):
    tokens, heads, width = queries.shape
    groups = keys.shape[1]
    feats = feature_weights.shape[3]
    rows = width // blocks
    vmem = pl.BlockSpec(memory_space=pltpu.VMEM)
    slot = pltpu.VMEM((heads, width + 8, feats), F32)
    query_grad, key_grad, value_grad, maps = pl.pallas_call(
        functools.partial(kernel, blocks, subs, heads // groups),
        out_shape=(
            jax.ShapeDtypeStruct((heads, tokens, width), BF16),
            jax.ShapeDtypeStruct((groups, tokens, width), BF16),
            jax.ShapeDtypeStruct((groups, tokens, width), BF16),
            jax.ShapeDtypeStruct((blocks, 2, heads, rows, feats), F32),
        ),
        in_specs=[vmem] * 5,
        out_specs=(vmem,) * 4,
        scratch_shapes=[
            pltpu.VMEM((heads, tokens, feats), BF16),
            pltpu.VMEM((heads, tokens, feats), BF16),
            pltpu.VMEM((heads, tokens, width), BF16),
            pltpu.VMEM((heads, tokens, 1), F32),
            pltpu.VMEM((heads, tokens, tokens), BF16),
            slot, slot, slot, slot,
            pltpu.VMEM((tokens, width), F32),
            pltpu.VMEM((tokens, width), F32),
            pltpu.SemaphoreType.DMA((heads,)),
            pltpu.SemaphoreType.DMA((heads,)),
            pltpu.SemaphoreType.DMA((heads,)),
            pltpu.SemaphoreType.DMA((heads,)),
        ],
        compiler_params=pltpu.CompilerParams(
            collective_id=0, has_side_effects=True, vmem_limit_bytes=56 * 1024 * 1024
        ),
    )(
        queries.transpose(1, 0, 2),
        keys.transpose(1, 0, 2),
        values.transpose(1, 0, 2),
        out_grad.transpose(1, 0, 2),
        feature_weights,
    )
    summed = lax.psum_scatter(maps, ("seq", "sub"), scatter_dimension=0, tiled=True)
    return (
        query_grad.transpose(1, 0, 2),
        key_grad.transpose(1, 0, 2),
        value_grad.transpose(1, 0, 2),
        summed[0].transpose(2, 0, 1, 3),
    )


def solution(mesh):
    subs = mesh.shape["sub"]
    blocks = mesh.shape["seq"] * subs
    rows = P(("grp", "seq", "sub"), "head", None)
    return jax.shard_map(
        functools.partial(shards, blocks, subs),
        mesh=mesh,
        in_specs=(rows, rows, rows, rows, P(None, "head", None, None)),
        out_specs=(rows, rows, rows, P(("grp", "seq", "sub"), None, "head", None)),
        check_vma=False,
    )
```

```python
import functools

import jax
import jax.numpy as jnp
from jax import lax
from jax.experimental import pallas as pl
from jax.experimental.pallas import tpu as pltpu
from jax.sharding import PartitionSpec as P

F32 = jnp.float32
BF16 = jnp.bfloat16
LAG = 2


def dot(left, right, left_dim, right_dim):
    return lax.dot_general(
        left, right, (((left_dim,), (right_dim,)), ((), ())), preferred_element_type=F32
    )


def softmax(logits):
    grown = jnp.exp(logits - jnp.max(logits, axis=1, keepdims=True))
    return grown * (1.0 / jnp.sum(grown, axis=1, keepdims=True))


def logit_grad(low, grad):
    feat = low.astype(F32)
    return (feat * (grad - jnp.sum(feat * grad, axis=1, keepdims=True))).astype(BF16)


def kernel(
    chips, subs, group_size, batch,
    q_ref, k_ref, v_ref, og_ref, w_ref,
    qg_ref, kg_ref, vg_ref, mg_ref,
    ql_ref, kl_ref, kf_ref,
    fwd_in, fwd_out, bwd_in, bwd_out, k_acc, v_acc,
    map_own, map_got, map_sum, map_far,
    fwd_send, fwd_recv, bwd_send, bwd_recv,
    pair_send, pair_recv, far_send, far_recv,
):
    heads, tokens, width = q_ref.shape
    feats = w_ref.shape[3]
    blocks = chips * subs
    chip = lax.axis_index("seq")
    core = lax.axis_index("sub")
    me = chip * subs + core
    before = jnp.maximum(me - 1, 0)
    after = jnp.minimum(me + 1, blocks - 1)
    batches = heads // batch

    def place(block):
        return {"seq": block // subs, "sub": block % subs}

    def send(src, dst, send_sem, recv_sem, target):
        return pltpu.make_async_remote_copy(
            src_ref=src, dst_ref=dst, send_sem=send_sem, recv_sem=recv_sem,
            device_id=target, device_id_type=pl.DeviceIdType.MESH,
        )

    def fwd_copy(h):
        return send(
            fwd_out.at[h], fwd_in.at[h], fwd_send.at[h], fwd_recv.at[h], place(after)
        )

    def bwd_copy(h):
        return send(
            bwd_out.at[h], bwd_in.at[h], bwd_send.at[h], bwd_recv.at[h], place(before)
        )

    def pair_copy(side, n):
        return send(
            map_own.at[side, n, 1 - core], map_got.at[side, n],
            pair_send.at[side, n], pair_recv.at[side, n],
            {"seq": chip, "sub": 1 - core},
        )

    def far_copy(side, n, hop):
        to = (chip + hop) % chips
        return send(
            map_sum.at[side, n, to], map_far.at[hop - 1, side, n],
            far_send.at[hop - 1, side, n], far_recv.at[hop - 1, side, n],
            {"seq": to, "sub": core},
        )

    barrier = pltpu.get_barrier_semaphore()
    for step in range(1, blocks):
        pl.semaphore_signal(
            barrier, inc=1, device_id=place((me + step) % blocks),
            device_id_type=pl.DeviceIdType.MESH,
        )
    pl.semaphore_wait(barrier, blocks - 1)

    @pl.when(me == 0)
    def _():
        fwd_in[...] = jnp.zeros_like(fwd_in)

    @pl.when(me == blocks - 1)
    def _():
        bwd_in[...] = jnp.zeros_like(bwd_in)

    fwd_lag = jnp.minimum(LAG * me, heads // 2)
    bwd_lag = jnp.minimum(LAG * (blocks - 1 - me), heads // 2)

    def fwd_step(h):
        @pl.when(me > 0)
        def _():
            fwd_copy(h).wait_recv()

        @pl.when(me < blocks - 1)
        def _():
            fwd_out[h] += fwd_in[h]
            fwd_copy(h).start()

    def bwd_step(h):
        @pl.when(me < blocks - 1)
        def _():
            bwd_copy(h).wait_recv()

        @pl.when(me > 0)
        def _():
            bwd_out[h] += bwd_in[h]
            bwd_copy(h).start()

    def put_map(side, h, product):
        n = h // batch
        rows = product.reshape(chips, subs, width // blocks, feats)
        for c in range(subs):
            map_own[side, n, c, :, h % batch] = rows[:, c]

        @pl.when(h % batch == batch - 1)
        def _():
            pair_copy(side, n).start()

    def spread_map(side, n):
        pair_copy(side, n).wait_recv()
        map_sum[side, n] = map_own[side, n, core] + map_got[side, n]
        for hop in range(1, chips):
            far_copy(side, n, hop).start()

    def features(h, carry):
        g = h // group_size
        ql_ref[h] = softmax(dot(q_ref[h], w_ref[0, h], 1, 0)).astype(BF16)
        key_low = softmax(dot(k_ref[g], w_ref[1, h], 1, 0)).astype(BF16)
        kl_ref[h] = key_low
        fwd_out[h, 0:width] = dot(v_ref[g], key_low, 0, 0)
        fwd_out[h, width:width + 8] = jnp.broadcast_to(
            jnp.sum(key_low.astype(F32), axis=0, keepdims=True), (8, feats)
        )

        @pl.when(h >= fwd_lag)
        def _():
            fwd_step(h - fwd_lag)

        return carry

    lax.fori_loop(0, heads, features, 0)

    def causal():
        rows = lax.broadcasted_iota(jnp.int32, (tokens, tokens), 0)
        return rows >= lax.broadcasted_iota(jnp.int32, (tokens, tokens), 1)

    def queries_side(h, carry):
        @pl.when(h < fwd_lag)
        def _():
            fwd_step(heads - fwd_lag + h)

        g = h // group_size
        query_low = ql_ref[h]
        key_low = kl_ref[h]
        value_rows = v_ref[g]
        state = fwd_in[h, 0:width].astype(BF16)
        state_z = fwd_in[h, width:width + 1]
        masked = jnp.where(causal(), dot(query_low, key_low, 1, 1), 0.0)
        weights = masked.astype(BF16)
        numerator = dot(weights, value_rows, 1, 0) + dot(query_low, state, 1, 1)
        query_round = query_low.astype(F32)
        denominator = jnp.sum(masked, axis=1, keepdims=True) + jnp.sum(
            query_round * state_z, axis=1, keepdims=True
        )
        grad = og_ref[h].astype(F32)
        numer_grad = (grad * (1.0 / denominator)).astype(BF16)
        denom_grad = -jnp.sum(grad * numerator, axis=1, keepdims=True) / (
            denominator * denominator
        )
        bwd_out[h, 0:width] = dot(numer_grad, query_low, 0, 0)
        bwd_out[h, width:width + 8] = jnp.broadcast_to(
            jnp.sum(query_round * denom_grad, axis=0, keepdims=True), (8, feats)
        )

        @pl.when(h >= bwd_lag)
        def _():
            bwd_step(h - bwd_lag)

        score_grad = jnp.where(
            causal(), dot(numer_grad, value_rows, 1, 1) + denom_grad, 0.0
        ).astype(BF16)
        query_feat_grad = (
            dot(score_grad, key_low, 1, 0)
            + dot(numer_grad, state, 1, 0)
            + denom_grad * state_z
        )
        query_logit_grad = logit_grad(query_low, query_feat_grad)
        qg_ref[h] = dot(query_logit_grad, w_ref[0, h], 1, 1).astype(BF16)
        put_map(0, h, dot(q_ref[h], query_logit_grad, 0, 0))
        kf_ref[h] = dot(score_grad, query_low, 0, 0)
        value_term = dot(weights, numer_grad, 0, 0)
        fresh = h % group_size == 0

        @pl.when(fresh)
        def _():
            v_acc[g] = value_term

        @pl.when(jnp.logical_not(fresh))
        def _():
            v_acc[g] += value_term

        @pl.when(jnp.logical_and(h % batch == 1, h >= batch))
        def _():
            spread_map(0, h // batch - 1)

        return carry

    lax.fori_loop(0, heads, queries_side, 0)

    def keys_side(h, carry):
        @pl.when(h < bwd_lag)
        def _():
            bwd_step(heads - bwd_lag + h)

        @pl.when(h == 1)
        def _():
            spread_map(0, batches - 1)

        g = h // group_size
        key_low = kl_ref[h]
        back = bwd_in[h, 0:width].astype(BF16)
        key_feat_grad = (
            kf_ref[h] + dot(v_ref[g], back, 1, 0) + bwd_in[h, width:width + 1]
        )
        key_logit_grad = logit_grad(key_low, key_feat_grad)
        put_map(1, h, dot(k_ref[g], key_logit_grad, 0, 0))
        key_term = dot(key_logit_grad, w_ref[1, h], 1, 1)
        v_acc[g] += dot(key_low, back, 1, 1)
        fresh = h % group_size == 0

        @pl.when(fresh)
        def _():
            k_acc[...] = key_term

        @pl.when(jnp.logical_not(fresh))
        def _():
            k_acc[...] += key_term

        @pl.when(h % group_size == group_size - 1)
        def _():
            kg_ref[g] = k_acc[...].astype(BF16)
            vg_ref[g] = v_acc[g].astype(BF16)

        @pl.when(jnp.logical_and(h % batch == 1, h >= batch))
        def _():
            spread_map(1, h // batch - 1)

        return carry

    lax.fori_loop(0, heads, keys_side, 0)
    spread_map(1, batches - 1)

    for side in range(2):
        def finish(n, carry):
            total = map_sum[side, n, chip]
            for hop in range(1, chips):
                far_copy(side, n, hop).wait_recv()
                total += map_far[hop - 1, side, n]
            mg_ref[side, n] = total
            pair_copy(side, n).wait_send()
            for hop in range(1, chips):
                far_copy(side, n, hop).wait_send()
            return carry

        lax.fori_loop(0, batches, finish, 0)

    def drain(h, carry):
        @pl.when(me < blocks - 1)
        def _():
            fwd_copy(h).wait_send()

        @pl.when(me > 0)
        def _():
            bwd_copy(h).wait_send()

        return carry

    lax.fori_loop(0, heads, drain, 0)


def shards(chips, subs, queries, keys, values, out_grad, feature_weights):
    tokens, heads, width = queries.shape
    groups = keys.shape[1]
    feats = feature_weights.shape[3]
    rows = width // (chips * subs)
    batch = 4
    batches = heads // batch
    vmem = pl.BlockSpec(memory_space=pltpu.VMEM)
    slot = pltpu.VMEM((heads, width + 8, feats), F32)
    pieces = (2, batches, chips, batch, rows, feats)
    query_grad, key_grad, value_grad, maps = pl.pallas_call(
        functools.partial(kernel, chips, subs, heads // groups, batch),
        out_shape=(
            jax.ShapeDtypeStruct((heads, tokens, width), BF16),
            jax.ShapeDtypeStruct((groups, tokens, width), BF16),
            jax.ShapeDtypeStruct((groups, tokens, width), BF16),
            jax.ShapeDtypeStruct((2, batches, batch, rows, feats), F32),
        ),
        in_specs=[vmem] * 5,
        out_specs=(vmem,) * 4,
        scratch_shapes=[
            pltpu.VMEM((heads, tokens, feats), BF16),
            pltpu.VMEM((heads, tokens, feats), BF16),
            pltpu.VMEM((heads, tokens, feats), F32),
            slot, slot, slot, slot,
            pltpu.VMEM((tokens, width), F32),
            pltpu.VMEM((groups, tokens, width), F32),
            pltpu.VMEM((2, batches, subs, chips, batch, rows, feats), F32),
            pltpu.VMEM(pieces, F32),
            pltpu.VMEM(pieces, F32),
            pltpu.VMEM((chips - 1, 2, batches, batch, rows, feats), F32),
        ]
        + [pltpu.SemaphoreType.DMA((heads,))] * 4
        + [pltpu.SemaphoreType.DMA((2, batches))] * 2
        + [pltpu.SemaphoreType.DMA((chips - 1, 2, batches))] * 2,
        compiler_params=pltpu.CompilerParams(
            collective_id=0, has_side_effects=True, vmem_limit_bytes=58 * 1024 * 1024
        ),
    )(
        queries.transpose(1, 0, 2),
        keys.transpose(1, 0, 2),
        values.transpose(1, 0, 2),
        out_grad.transpose(1, 0, 2),
        feature_weights,
    )
    return (
        query_grad.transpose(1, 0, 2),
        key_grad.transpose(1, 0, 2),
        value_grad.transpose(1, 0, 2),
        maps.reshape(2, heads, rows, feats).transpose(2, 0, 1, 3),
    )


def solution(mesh):
    chips = mesh.shape["seq"]
    subs = mesh.shape["sub"]
    rows = P(("grp", "seq", "sub"), "head", None)
    return jax.shard_map(
        functools.partial(shards, chips, subs),
        mesh=mesh,
        in_specs=(rows, rows, rows, rows, P(None, "head", None, None)),
        out_specs=(rows, rows, rows, P(("grp", "seq", "sub"), None, "head", None)),
        check_vma=False,
    )
```

```python
import functools

import jax
import jax.numpy as jnp
from jax import lax
from jax.experimental import pallas as pl
from jax.experimental.pallas import tpu as pltpu
from jax.sharding import PartitionSpec as P

F32 = jnp.float32
BF16 = jnp.bfloat16
PAIR = 2


def dot(left, right, left_dim, right_dim):
    return lax.dot_general(
        left, right, (((left_dim,), (right_dim,)), ((), ())), preferred_element_type=F32
    )


def softmax(logits):
    grown = jnp.exp(logits - jnp.max(logits, axis=1, keepdims=True))
    return grown * (1.0 / jnp.sum(grown, axis=1, keepdims=True))


def logit_grad(low, grad):
    feat = low.astype(F32)
    return (feat * (grad - jnp.sum(feat * grad, axis=1, keepdims=True))).astype(BF16)


def kernel(
    chips, subs, group_size, batch,
    q_ref, k_ref, v_ref, og_ref, w_ref,
    qg_ref, kg_ref, vg_ref, mg_ref,
    ql_ref, kl_ref, kf_ref,
    fwd_in, fwd_out, bwd_in, bwd_out, k_acc, v_acc,
    map_own, map_got, map_sum, map_far,
    fwd_send, fwd_recv, bwd_send, bwd_recv,
    pair_send, pair_recv, far_send, far_recv,
):
    heads, tokens, width = q_ref.shape
    feats = w_ref.shape[3]
    blocks = chips * subs
    chip = lax.axis_index("seq")
    core = lax.axis_index("sub")
    me = chip * subs + core
    before = jnp.maximum(me - 1, 0)
    after = jnp.minimum(me + 1, blocks - 1)
    batches = heads // batch

    def place(block):
        return {"seq": block // subs, "sub": block % subs}

    def send(src, dst, send_sem, recv_sem, target):
        return pltpu.make_async_remote_copy(
            src_ref=src, dst_ref=dst, send_sem=send_sem, recv_sem=recv_sem,
            device_id=target, device_id_type=pl.DeviceIdType.MESH,
        )

    def pair(p):
        return pl.ds(p * PAIR, PAIR)

    def fwd_copy(h):
        return send(
            fwd_out.at[pair(h)], fwd_in.at[pair(h)], fwd_send.at[h], fwd_recv.at[h], place(after)
        )

    def bwd_copy(h):
        return send(
            bwd_out.at[pair(h)], bwd_in.at[pair(h)], bwd_send.at[h], bwd_recv.at[h], place(before)
        )

    def pair_copy(side, n):
        return send(
            map_own.at[side, n, 1 - core], map_got.at[side, n],
            pair_send.at[side, n], pair_recv.at[side, n],
            {"seq": chip, "sub": 1 - core},
        )

    def far_copy(side, n, hop):
        to = (chip + hop) % chips
        return send(
            map_sum.at[side, n, to], map_far.at[hop - 1, side, n],
            far_send.at[hop - 1, side, n], far_recv.at[hop - 1, side, n],
            {"seq": to, "sub": core},
        )

    barrier = pltpu.get_barrier_semaphore()
    for step in range(1, blocks):
        pl.semaphore_signal(
            barrier, inc=1, device_id=place((me + step) % blocks),
            device_id_type=pl.DeviceIdType.MESH,
        )
    pl.semaphore_wait(barrier, blocks - 1)

    @pl.when(me == 0)
    def _():
        fwd_in[...] = jnp.zeros_like(fwd_in)

    @pl.when(me == blocks - 1)
    def _():
        bwd_in[...] = jnp.zeros_like(bwd_in)

    pairs = heads // PAIR
    turns = batch // PAIR
    fwd_lag = jnp.minimum(me, pairs // 2)
    bwd_lag = jnp.minimum(blocks - 1 - me, pairs // 2)
    k_acc[...] = jnp.zeros_like(k_acc)
    v_acc[...] = jnp.zeros_like(v_acc)

    def fwd_step(h):
        @pl.when(me > 0)
        def _():
            fwd_copy(h).wait_recv()

        @pl.when(me < blocks - 1)
        def _():
            fwd_out[pair(h)] += fwd_in[pair(h)]
            fwd_copy(h).start()

    def bwd_step(h):
        @pl.when(me < blocks - 1)
        def _():
            bwd_copy(h).wait_recv()

        @pl.when(me > 0)
        def _():
            bwd_out[pair(h)] += bwd_in[pair(h)]
            bwd_copy(h).start()

    def put_map(side, h, product):
        rows = product.reshape(chips, subs, width // blocks, feats)
        for c in range(subs):
            map_own[side, h // batch, c, :, h % batch] = rows[:, c]

    def spread_map(side, n):
        pair_copy(side, n).wait_recv()
        map_sum[side, n] = map_own[side, n, core] + map_got[side, n]
        for hop in range(1, chips):
            far_copy(side, n, hop).start()

    def send_map(side, p):
        @pl.when(p % turns == turns - 1)
        def _():
            pair_copy(side, p // turns).start()

        @pl.when(jnp.logical_and(p % turns == 0, p >= turns))
        def _():
            spread_map(side, p // turns - 1)

    def halves(both):
        return [both[:, u * feats:(u + 1) * feats] for u in range(PAIR)]

    def side_by_side(parts):
        return jnp.concatenate(parts, axis=1)

    def features(p, carry):
        heads_now = [p * PAIR + u for u in range(PAIR)]
        g = p * PAIR // group_size
        queries_low = [
            softmax(dot(q_ref[h], w_ref[0, h], 1, 0)).astype(BF16) for h in heads_now
        ]
        logits = dot(k_ref[g], side_by_side([w_ref[1, h] for h in heads_now]), 1, 0)
        keys_low = [softmax(part).astype(BF16) for part in halves(logits)]
        own = halves(dot(v_ref[g], side_by_side(keys_low), 0, 0))
        for u, h in enumerate(heads_now):
            ql_ref[h] = queries_low[u]
            kl_ref[h] = keys_low[u]
            fwd_out[h, 0:width] = own[u]
            fwd_out[h, width:width + 8] = jnp.broadcast_to(
                jnp.sum(keys_low[u].astype(F32), axis=0, keepdims=True), (8, feats)
            )

        @pl.when(p >= fwd_lag)
        def _():
            fwd_step(p - fwd_lag)

        return carry

    lax.fori_loop(0, pairs, features, 0)

    def causal():
        rows = lax.broadcasted_iota(jnp.int32, (tokens, tokens), 0)
        return rows >= lax.broadcasted_iota(jnp.int32, (tokens, tokens), 1)

    def queries_side(p, carry):
        @pl.when(p < fwd_lag)
        def _():
            fwd_step(pairs - fwd_lag + p)

        heads_now = [p * PAIR + u for u in range(PAIR)]
        g = p * PAIR // group_size
        value_rows = v_ref[g]
        below = causal()
        done = []
        for h in heads_now:
            query_low = ql_ref[h]
            key_low = kl_ref[h]
            state = fwd_in[h, 0:width].astype(BF16)
            state_z = fwd_in[h, width:width + 1]
            masked = jnp.where(below, dot(query_low, key_low, 1, 1), 0.0)
            weights = masked.astype(BF16)
            numerator = dot(weights, value_rows, 1, 0) + dot(query_low, state, 1, 1)
            query_round = query_low.astype(F32)
            denominator = jnp.sum(masked, axis=1, keepdims=True) + jnp.sum(
                query_round * state_z, axis=1, keepdims=True
            )
            grad = og_ref[h].astype(F32)
            numer_grad = (grad * (1.0 / denominator)).astype(BF16)
            denom_grad = -jnp.sum(grad * numerator, axis=1, keepdims=True) / (
                denominator * denominator
            )
            own = dot(numer_grad, query_low, 0, 0)
            own_z = jnp.sum(query_round * denom_grad, axis=0, keepdims=True)
            score_grad = jnp.where(
                below, dot(numer_grad, value_rows, 1, 1) + denom_grad, 0.0
            ).astype(BF16)
            query_feat_grad = (
                dot(score_grad, key_low, 1, 0)
                + dot(numer_grad, state, 1, 0)
                + denom_grad * state_z
            )
            query_logit_grad = logit_grad(query_low, query_feat_grad)
            query_grad = dot(query_logit_grad, w_ref[0, h], 1, 1).astype(BF16)
            map_term = dot(q_ref[h], query_logit_grad, 0, 0)
            key_term = dot(score_grad, query_low, 0, 0)
            done.append(
                (own, own_z, query_grad, map_term, key_term, weights, numer_grad)
            )
        value_term = dot(
            jnp.concatenate([item[5] for item in done], axis=0),
            jnp.concatenate([item[6] for item in done], axis=0), 0, 0,
        )
        for h, item in zip(heads_now, done):
            bwd_out[h, 0:width] = item[0]
            bwd_out[h, width:width + 8] = jnp.broadcast_to(item[1], (8, feats))
            qg_ref[h] = item[2]
            put_map(0, h, item[3])
            kf_ref[h] = item[4]
        v_acc[g] += value_term

        @pl.when(p >= bwd_lag)
        def _():
            bwd_step(p - bwd_lag)

        send_map(0, p)
        return carry

    lax.fori_loop(0, pairs, queries_side, 0)

    def keys_side(p, carry):
        @pl.when(p < bwd_lag)
        def _():
            bwd_step(pairs - bwd_lag + p)

        @pl.when(p == 0)
        def _():
            spread_map(0, batches - 1)

        heads_now = [p * PAIR + u for u in range(PAIR)]
        g = p * PAIR // group_size
        keys_low = [kl_ref[h] for h in heads_now]
        back = side_by_side([bwd_in[h, 0:width].astype(BF16) for h in heads_now])
        far = halves(dot(v_ref[g], back, 1, 0))
        logit_grads = side_by_side([
            logit_grad(keys_low[u], kf_ref[h] + far[u] + bwd_in[h, width:width + 1])
            for u, h in enumerate(heads_now)
        ])
        maps = halves(dot(k_ref[g], logit_grads, 0, 0))
        key_term = dot(
            logit_grads, side_by_side([w_ref[1, h] for h in heads_now]), 1, 1
        )
        value_term = dot(side_by_side(keys_low), back, 1, 1)
        for u, h in enumerate(heads_now):
            put_map(1, h, maps[u])
        k_acc[g] += key_term
        v_acc[g] += value_term
        send_map(1, p)
        return carry

    lax.fori_loop(0, pairs, keys_side, 0)
    spread_map(1, batches - 1)
    kg_ref[...] = k_acc[...].astype(BF16)
    vg_ref[...] = v_acc[...].astype(BF16)

    for side in range(2):
        def finish(n, carry):
            total = map_sum[side, n, chip]
            for hop in range(1, chips):
                far_copy(side, n, hop).wait_recv()
                total += map_far[hop - 1, side, n]
            mg_ref[side, n] = total
            pair_copy(side, n).wait_send()
            for hop in range(1, chips):
                far_copy(side, n, hop).wait_send()
            return carry

        lax.fori_loop(0, batches, finish, 0)

    def drain(h, carry):
        @pl.when(me < blocks - 1)
        def _():
            fwd_copy(h).wait_send()

        @pl.when(me > 0)
        def _():
            bwd_copy(h).wait_send()

        return carry

    lax.fori_loop(0, pairs, drain, 0)


def shards(chips, subs, queries, keys, values, out_grad, feature_weights):
    tokens, heads, width = queries.shape
    groups = keys.shape[1]
    feats = feature_weights.shape[3]
    rows = width // (chips * subs)
    batch = 4
    batches = heads // batch
    vmem = pl.BlockSpec(memory_space=pltpu.VMEM)
    slot = pltpu.VMEM((heads, width + 8, feats), F32)
    pieces = (2, batches, chips, batch, rows, feats)
    query_grad, key_grad, value_grad, maps = pl.pallas_call(
        functools.partial(kernel, chips, subs, heads // groups, batch),
        out_shape=(
            jax.ShapeDtypeStruct((heads, tokens, width), BF16),
            jax.ShapeDtypeStruct((groups, tokens, width), BF16),
            jax.ShapeDtypeStruct((groups, tokens, width), BF16),
            jax.ShapeDtypeStruct((2, batches, batch, rows, feats), F32),
        ),
        in_specs=[vmem] * 5,
        out_specs=(vmem,) * 4,
        scratch_shapes=[
            pltpu.VMEM((heads, tokens, feats), BF16),
            pltpu.VMEM((heads, tokens, feats), BF16),
            pltpu.VMEM((heads, tokens, feats), F32),
            slot, slot, slot, slot,
            pltpu.VMEM((groups, tokens, width), F32),
            pltpu.VMEM((groups, tokens, width), F32),
            pltpu.VMEM((2, batches, subs, chips, batch, rows, feats), F32),
            pltpu.VMEM(pieces, F32),
            pltpu.VMEM(pieces, F32),
            pltpu.VMEM((chips - 1, 2, batches, batch, rows, feats), F32),
        ]
        + [pltpu.SemaphoreType.DMA((heads // PAIR,))] * 4
        + [pltpu.SemaphoreType.DMA((2, batches))] * 2
        + [pltpu.SemaphoreType.DMA((chips - 1, 2, batches))] * 2,
        compiler_params=pltpu.CompilerParams(
            collective_id=0, has_side_effects=True, vmem_limit_bytes=58 * 1024 * 1024
        ),
    )(
        queries.transpose(1, 0, 2),
        keys.transpose(1, 0, 2),
        values.transpose(1, 0, 2),
        out_grad.transpose(1, 0, 2),
        feature_weights,
    )
    return (
        query_grad.transpose(1, 0, 2),
        key_grad.transpose(1, 0, 2),
        value_grad.transpose(1, 0, 2),
        maps.reshape(2, heads, rows, feats).transpose(2, 0, 1, 3),
    )


def solution(mesh):
    chips = mesh.shape["seq"]
    subs = mesh.shape["sub"]
    rows = P(("grp", "seq", "sub"), "head", None)
    return jax.shard_map(
        functools.partial(shards, chips, subs),
        mesh=mesh,
        in_specs=(rows, rows, rows, rows, P(None, "head", None, None)),
        out_specs=(rows, rows, rows, P(("grp", "seq", "sub"), None, "head", None)),
        check_vma=False,
    )
```

```python
import functools

import jax
import jax.numpy as jnp
from jax import lax
from jax.experimental import pallas as pl
from jax.experimental.pallas import tpu as pltpu
from jax.sharding import PartitionSpec as P

F32 = jnp.float32
BF16 = jnp.bfloat16
LAG = 1


def dot(left, right, left_dim, right_dim):
    return lax.dot_general(
        left, right, (((left_dim,), (right_dim,)), ((), ())), preferred_element_type=F32
    )


def softmax(logits):
    grown = jnp.exp(logits - jnp.max(logits, axis=1, keepdims=True))
    return grown * (1.0 / jnp.sum(grown, axis=1, keepdims=True))


def logit_grad(low, grad):
    feat = low.astype(F32)
    return (feat * (grad - jnp.sum(feat * grad, axis=1, keepdims=True))).astype(BF16)


def kernel(
    chips, subs, group_size, batch,
    q_ref, k_ref, v_ref, og_ref, w_ref,
    qg_ref, kg_ref, vg_ref, mg_ref,
    ql_ref, kl_ref, kf_ref,
    fwd_in, fwd_out, bwd_in, bwd_out, k_acc, v_acc,
    map_own, map_got, map_sum, map_far,
    fwd_send, fwd_recv, bwd_send, bwd_recv,
    pair_send, pair_recv, far_send, far_recv,
):
    heads, tokens, width = q_ref.shape
    feats = w_ref.shape[3]
    blocks = chips * subs
    chip = lax.axis_index("seq")
    core = lax.axis_index("sub")
    me = chip * subs + core
    before = jnp.maximum(me - 1, 0)
    after = jnp.minimum(me + 1, blocks - 1)
    batches = heads // batch

    def place(block):
        return {"seq": block // subs, "sub": block % subs}

    def send(src, dst, send_sem, recv_sem, target):
        return pltpu.make_async_remote_copy(
            src_ref=src, dst_ref=dst, send_sem=send_sem, recv_sem=recv_sem,
            device_id=target, device_id_type=pl.DeviceIdType.MESH,
        )

    def fwd_copy(h):
        return send(
            fwd_out.at[h], fwd_in.at[h], fwd_send.at[h], fwd_recv.at[h], place(after)
        )

    def bwd_copy(h):
        return send(
            bwd_out.at[h], bwd_in.at[h], bwd_send.at[h], bwd_recv.at[h], place(before)
        )

    def pair_copy(side, n):
        return send(
            map_own.at[side, n, 1 - core], map_got.at[side, n],
            pair_send.at[side, n], pair_recv.at[side, n],
            {"seq": chip, "sub": 1 - core},
        )

    def far_copy(side, n, hop):
        to = (chip + hop) % chips
        return send(
            map_sum.at[side, n, to], map_far.at[hop - 1, side, n],
            far_send.at[hop - 1, side, n], far_recv.at[hop - 1, side, n],
            {"seq": to, "sub": core},
        )

    barrier = pltpu.get_barrier_semaphore()
    for step in range(1, blocks):
        pl.semaphore_signal(
            barrier, inc=1, device_id=place((me + step) % blocks),
            device_id_type=pl.DeviceIdType.MESH,
        )
    pl.semaphore_wait(barrier, blocks - 1)

    @pl.when(me == 0)
    def _():
        fwd_in[...] = jnp.zeros_like(fwd_in)

    @pl.when(me == blocks - 1)
    def _():
        bwd_in[...] = jnp.zeros_like(bwd_in)

    fwd_lag = jnp.minimum(LAG * me, heads // 2)
    bwd_lag = jnp.minimum(LAG * (blocks - 1 - me), heads // 2)

    def fwd_step(h):
        @pl.when(me > 0)
        def _():
            fwd_copy(h).wait_recv()

        @pl.when(me < blocks - 1)
        def _():
            fwd_out[h] += fwd_in[h]
            fwd_copy(h).start()

    def bwd_step(h):
        @pl.when(me < blocks - 1)
        def _():
            bwd_copy(h).wait_recv()

        @pl.when(me > 0)
        def _():
            bwd_out[h] += bwd_in[h]
            bwd_copy(h).start()

    def put_map(side, h, product):
        n = h // batch
        rows = product.reshape(chips, subs, width // blocks, feats)
        for c in range(subs):
            map_own[side, n, c, :, h % batch] = rows[:, c]

        @pl.when(h % batch == batch - 1)
        def _():
            pair_copy(side, n).start()

    def spread_map(side, n):
        pair_copy(side, n).wait_recv()
        map_sum[side, n] = map_own[side, n, core] + map_got[side, n]
        for hop in range(1, chips):
            far_copy(side, n, hop).start()

    def features(h, carry):
        g = h // group_size
        ql_ref[h] = softmax(dot(q_ref[h], w_ref[0, h], 1, 0)).astype(BF16)
        key_low = softmax(dot(k_ref[g], w_ref[1, h], 1, 0)).astype(BF16)
        kl_ref[h] = key_low
        fwd_out[h, 0:width] = dot(v_ref[g], key_low, 0, 0)
        fwd_out[h, width:width + 8] = jnp.broadcast_to(
            jnp.sum(key_low.astype(F32), axis=0, keepdims=True), (8, feats)
        )

        @pl.when(h >= fwd_lag)
        def _():
            fwd_step(h - fwd_lag)

        return carry

    lax.fori_loop(0, heads, features, 0)

    def causal():
        rows = lax.broadcasted_iota(jnp.int32, (tokens, tokens), 0)
        return rows >= lax.broadcasted_iota(jnp.int32, (tokens, tokens), 1)

    def queries_side(h, carry):
        @pl.when(h < fwd_lag)
        def _():
            fwd_step(heads - fwd_lag + h)

        g = h // group_size
        query_low = ql_ref[h]
        key_low = kl_ref[h]
        value_rows = v_ref[g]
        state = fwd_in[h, 0:width].astype(BF16)
        state_z = fwd_in[h, width:width + 1]
        masked = jnp.where(causal(), dot(query_low, key_low, 1, 1), 0.0)
        weights = masked.astype(BF16)
        numerator = dot(weights, value_rows, 1, 0) + dot(query_low, state, 1, 1)
        query_round = query_low.astype(F32)
        denominator = jnp.sum(masked, axis=1, keepdims=True) + jnp.sum(
            query_round * state_z, axis=1, keepdims=True
        )
        grad = og_ref[h].astype(F32)
        numer_grad = (grad * (1.0 / denominator)).astype(BF16)
        denom_grad = -jnp.sum(grad * numerator, axis=1, keepdims=True) / (
            denominator * denominator
        )
        bwd_out[h, 0:width] = dot(numer_grad, query_low, 0, 0)
        bwd_out[h, width:width + 8] = jnp.broadcast_to(
            jnp.sum(query_round * denom_grad, axis=0, keepdims=True), (8, feats)
        )

        @pl.when(h >= bwd_lag)
        def _():
            bwd_step(h - bwd_lag)

        score_grad = jnp.where(
            causal(), dot(numer_grad, value_rows, 1, 1) + denom_grad, 0.0
        ).astype(BF16)
        query_feat_grad = (
            dot(score_grad, key_low, 1, 0)
            + dot(numer_grad, state, 1, 0)
            + denom_grad * state_z
        )
        query_logit_grad = logit_grad(query_low, query_feat_grad)
        qg_ref[h] = dot(query_logit_grad, w_ref[0, h], 1, 1).astype(BF16)
        put_map(0, h, dot(q_ref[h], query_logit_grad, 0, 0))
        kf_ref[h] = dot(score_grad, query_low, 0, 0)
        value_term = dot(weights, numer_grad, 0, 0)
        fresh = h % group_size == 0

        @pl.when(fresh)
        def _():
            v_acc[g] = value_term

        @pl.when(jnp.logical_not(fresh))
        def _():
            v_acc[g] += value_term

        @pl.when(jnp.logical_and(h % batch == 1, h >= batch))
        def _():
            spread_map(0, h // batch - 1)

        return carry

    lax.fori_loop(0, heads, queries_side, 0)

    def keys_side(h, carry):
        @pl.when(h < bwd_lag)
        def _():
            bwd_step(heads - bwd_lag + h)

        @pl.when(h == 1)
        def _():
            spread_map(0, batches - 1)

        g = h // group_size
        key_low = kl_ref[h]
        back = bwd_in[h, 0:width].astype(BF16)
        key_feat_grad = (
            kf_ref[h] + dot(v_ref[g], back, 1, 0) + bwd_in[h, width:width + 1]
        )
        key_logit_grad = logit_grad(key_low, key_feat_grad)
        put_map(1, h, dot(k_ref[g], key_logit_grad, 0, 0))
        key_term = dot(key_logit_grad, w_ref[1, h], 1, 1)
        v_acc[g] += dot(key_low, back, 1, 1)
        fresh = h % group_size == 0

        @pl.when(fresh)
        def _():
            k_acc[...] = key_term

        @pl.when(jnp.logical_not(fresh))
        def _():
            k_acc[...] += key_term

        @pl.when(h % group_size == group_size - 1)
        def _():
            kg_ref[g] = k_acc[...].astype(BF16)
            vg_ref[g] = v_acc[g].astype(BF16)

        @pl.when(jnp.logical_and(h % batch == 1, h >= batch))
        def _():
            spread_map(1, h // batch - 1)

        return carry

    lax.fori_loop(0, heads, keys_side, 0)
    spread_map(1, batches - 1)

    for side in range(2):
        def finish(n, carry):
            total = map_sum[side, n, chip]
            for hop in range(1, chips):
                far_copy(side, n, hop).wait_recv()
                total += map_far[hop - 1, side, n]
            mg_ref[side, n] = total
            pair_copy(side, n).wait_send()
            for hop in range(1, chips):
                far_copy(side, n, hop).wait_send()
            return carry

        lax.fori_loop(0, batches, finish, 0)

    def drain(h, carry):
        @pl.when(me < blocks - 1)
        def _():
            fwd_copy(h).wait_send()

        @pl.when(me > 0)
        def _():
            bwd_copy(h).wait_send()

        return carry

    lax.fori_loop(0, heads, drain, 0)


def shards(chips, subs, queries, keys, values, out_grad, feature_weights):
    tokens, heads, width = queries.shape
    groups = keys.shape[1]
    feats = feature_weights.shape[3]
    rows = width // (chips * subs)
    batch = 4
    batches = heads // batch
    vmem = pl.BlockSpec(memory_space=pltpu.VMEM)
    slot = pltpu.VMEM((heads, width + 8, feats), F32)
    pieces = (2, batches, chips, batch, rows, feats)
    query_grad, key_grad, value_grad, maps = pl.pallas_call(
        functools.partial(kernel, chips, subs, heads // groups, batch),
        out_shape=(
            jax.ShapeDtypeStruct((heads, tokens, width), BF16),
            jax.ShapeDtypeStruct((groups, tokens, width), BF16),
            jax.ShapeDtypeStruct((groups, tokens, width), BF16),
            jax.ShapeDtypeStruct((2, batches, batch, rows, feats), F32),
        ),
        in_specs=[vmem] * 5,
        out_specs=(vmem,) * 4,
        scratch_shapes=[
            pltpu.VMEM((heads, tokens, feats), BF16),
            pltpu.VMEM((heads, tokens, feats), BF16),
            pltpu.VMEM((heads, tokens, feats), F32),
            slot, slot, slot, slot,
            pltpu.VMEM((tokens, width), F32),
            pltpu.VMEM((groups, tokens, width), F32),
            pltpu.VMEM((2, batches, subs, chips, batch, rows, feats), F32),
            pltpu.VMEM(pieces, F32),
            pltpu.VMEM(pieces, F32),
            pltpu.VMEM((chips - 1, 2, batches, batch, rows, feats), F32),
        ]
        + [pltpu.SemaphoreType.DMA((heads,))] * 4
        + [pltpu.SemaphoreType.DMA((2, batches))] * 2
        + [pltpu.SemaphoreType.DMA((chips - 1, 2, batches))] * 2,
        compiler_params=pltpu.CompilerParams(
            collective_id=0, has_side_effects=True, vmem_limit_bytes=58 * 1024 * 1024
        ),
    )(
        queries.transpose(1, 0, 2),
        keys.transpose(1, 0, 2),
        values.transpose(1, 0, 2),
        out_grad.transpose(1, 0, 2),
        feature_weights,
    )
    return (
        query_grad.transpose(1, 0, 2),
        key_grad.transpose(1, 0, 2),
        value_grad.transpose(1, 0, 2),
        maps.reshape(2, heads, rows, feats).transpose(2, 0, 1, 3),
    )


def solution(mesh):
    chips = mesh.shape["seq"]
    subs = mesh.shape["sub"]
    rows = P(("grp", "seq", "sub"), "head", None)
    return jax.shard_map(
        functools.partial(shards, chips, subs),
        mesh=mesh,
        in_specs=(rows, rows, rows, rows, P(None, "head", None, None)),
        out_specs=(rows, rows, rows, P(("grp", "seq", "sub"), None, "head", None)),
        check_vma=False,
    )
```

```python
import functools

import jax
import jax.numpy as jnp
from jax import lax
from jax.experimental import pallas as pl
from jax.experimental.pallas import tpu as pltpu
from jax.sharding import PartitionSpec as P

F32 = jnp.float32
BF16 = jnp.bfloat16
LAG = 3


def dot(left, right, left_dim, right_dim):
    return lax.dot_general(
        left, right, (((left_dim,), (right_dim,)), ((), ())), preferred_element_type=F32
    )


def softmax(logits):
    grown = jnp.exp(logits - jnp.max(logits, axis=1, keepdims=True))
    return grown * (1.0 / jnp.sum(grown, axis=1, keepdims=True))


def logit_grad(low, grad):
    feat = low.astype(F32)
    return (feat * (grad - jnp.sum(feat * grad, axis=1, keepdims=True))).astype(BF16)


def kernel(
    chips, subs, group_size, batch,
    q_ref, k_ref, v_ref, og_ref, w_ref,
    qg_ref, kg_ref, vg_ref, mg_ref,
    ql_ref, kl_ref, kf_ref,
    fwd_in, fwd_out, bwd_in, bwd_out, k_acc, v_acc,
    map_own, map_got, map_sum, map_far,
    fwd_send, fwd_recv, bwd_send, bwd_recv,
    pair_send, pair_recv, far_send, far_recv,
):
    heads, tokens, width = q_ref.shape
    feats = w_ref.shape[3]
    blocks = chips * subs
    chip = lax.axis_index("seq")
    core = lax.axis_index("sub")
    me = chip * subs + core
    before = jnp.maximum(me - 1, 0)
    after = jnp.minimum(me + 1, blocks - 1)
    batches = heads // batch

    def place(block):
        return {"seq": block // subs, "sub": block % subs}

    def send(src, dst, send_sem, recv_sem, target):
        return pltpu.make_async_remote_copy(
            src_ref=src, dst_ref=dst, send_sem=send_sem, recv_sem=recv_sem,
            device_id=target, device_id_type=pl.DeviceIdType.MESH,
        )

    def fwd_copy(h):
        return send(
            fwd_out.at[h], fwd_in.at[h], fwd_send.at[h], fwd_recv.at[h], place(after)
        )

    def bwd_copy(h):
        return send(
            bwd_out.at[h], bwd_in.at[h], bwd_send.at[h], bwd_recv.at[h], place(before)
        )

    def pair_copy(side, n):
        return send(
            map_own.at[side, n, 1 - core], map_got.at[side, n],
            pair_send.at[side, n], pair_recv.at[side, n],
            {"seq": chip, "sub": 1 - core},
        )

    def far_copy(side, n, hop):
        to = (chip + hop) % chips
        return send(
            map_sum.at[side, n, to], map_far.at[hop - 1, side, n],
            far_send.at[hop - 1, side, n], far_recv.at[hop - 1, side, n],
            {"seq": to, "sub": core},
        )

    barrier = pltpu.get_barrier_semaphore()
    for step in range(1, blocks):
        pl.semaphore_signal(
            barrier, inc=1, device_id=place((me + step) % blocks),
            device_id_type=pl.DeviceIdType.MESH,
        )
    pl.semaphore_wait(barrier, blocks - 1)

    @pl.when(me == 0)
    def _():
        fwd_in[...] = jnp.zeros_like(fwd_in)

    @pl.when(me == blocks - 1)
    def _():
        bwd_in[...] = jnp.zeros_like(bwd_in)

    fwd_lag = jnp.minimum(LAG * me, heads // 2)
    bwd_lag = jnp.minimum(LAG * (blocks - 1 - me), heads // 2)

    def fwd_step(h):
        @pl.when(me > 0)
        def _():
            fwd_copy(h).wait_recv()

        @pl.when(me < blocks - 1)
        def _():
            fwd_out[h] += fwd_in[h]
            fwd_copy(h).start()

    def bwd_step(h):
        @pl.when(me < blocks - 1)
        def _():
            bwd_copy(h).wait_recv()

        @pl.when(me > 0)
        def _():
            bwd_out[h] += bwd_in[h]
            bwd_copy(h).start()

    def put_map(side, h, product):
        n = h // batch
        rows = product.reshape(chips, subs, width // blocks, feats)
        for c in range(subs):
            map_own[side, n, c, :, h % batch] = rows[:, c]

        @pl.when(h % batch == batch - 1)
        def _():
            pair_copy(side, n).start()

    def spread_map(side, n):
        pair_copy(side, n).wait_recv()
        map_sum[side, n] = map_own[side, n, core] + map_got[side, n]
        for hop in range(1, chips):
            far_copy(side, n, hop).start()

    def features(h, carry):
        g = h // group_size
        ql_ref[h] = softmax(dot(q_ref[h], w_ref[0, h], 1, 0)).astype(BF16)
        key_low = softmax(dot(k_ref[g], w_ref[1, h], 1, 0)).astype(BF16)
        kl_ref[h] = key_low
        fwd_out[h, 0:width] = dot(v_ref[g], key_low, 0, 0)
        fwd_out[h, width:width + 8] = jnp.broadcast_to(
            jnp.sum(key_low.astype(F32), axis=0, keepdims=True), (8, feats)
        )

        @pl.when(h >= fwd_lag)
        def _():
            fwd_step(h - fwd_lag)

        return carry

    lax.fori_loop(0, heads, features, 0)

    def causal():
        rows = lax.broadcasted_iota(jnp.int32, (tokens, tokens), 0)
        return rows >= lax.broadcasted_iota(jnp.int32, (tokens, tokens), 1)

    def queries_side(h, carry):
        @pl.when(h < fwd_lag)
        def _():
            fwd_step(heads - fwd_lag + h)

        g = h // group_size
        query_low = ql_ref[h]
        key_low = kl_ref[h]
        value_rows = v_ref[g]
        state = fwd_in[h, 0:width].astype(BF16)
        state_z = fwd_in[h, width:width + 1]
        masked = jnp.where(causal(), dot(query_low, key_low, 1, 1), 0.0)
        weights = masked.astype(BF16)
        numerator = dot(weights, value_rows, 1, 0) + dot(query_low, state, 1, 1)
        query_round = query_low.astype(F32)
        denominator = jnp.sum(masked, axis=1, keepdims=True) + jnp.sum(
            query_round * state_z, axis=1, keepdims=True
        )
        grad = og_ref[h].astype(F32)
        numer_grad = (grad * (1.0 / denominator)).astype(BF16)
        denom_grad = -jnp.sum(grad * numerator, axis=1, keepdims=True) / (
            denominator * denominator
        )
        bwd_out[h, 0:width] = dot(numer_grad, query_low, 0, 0)
        bwd_out[h, width:width + 8] = jnp.broadcast_to(
            jnp.sum(query_round * denom_grad, axis=0, keepdims=True), (8, feats)
        )

        @pl.when(h >= bwd_lag)
        def _():
            bwd_step(h - bwd_lag)

        score_grad = jnp.where(
            causal(), dot(numer_grad, value_rows, 1, 1) + denom_grad, 0.0
        ).astype(BF16)
        query_feat_grad = (
            dot(score_grad, key_low, 1, 0)
            + dot(numer_grad, state, 1, 0)
            + denom_grad * state_z
        )
        query_logit_grad = logit_grad(query_low, query_feat_grad)
        qg_ref[h] = dot(query_logit_grad, w_ref[0, h], 1, 1).astype(BF16)
        put_map(0, h, dot(q_ref[h], query_logit_grad, 0, 0))
        kf_ref[h] = dot(score_grad, query_low, 0, 0)
        value_term = dot(weights, numer_grad, 0, 0)
        fresh = h % group_size == 0

        @pl.when(fresh)
        def _():
            v_acc[g] = value_term

        @pl.when(jnp.logical_not(fresh))
        def _():
            v_acc[g] += value_term

        @pl.when(jnp.logical_and(h % batch == 1, h >= batch))
        def _():
            spread_map(0, h // batch - 1)

        return carry

    lax.fori_loop(0, heads, queries_side, 0)

    def keys_side(h, carry):
        @pl.when(h < bwd_lag)
        def _():
            bwd_step(heads - bwd_lag + h)

        @pl.when(h == 1)
        def _():
            spread_map(0, batches - 1)

        g = h // group_size
        key_low = kl_ref[h]
        back = bwd_in[h, 0:width].astype(BF16)
        key_feat_grad = (
            kf_ref[h] + dot(v_ref[g], back, 1, 0) + bwd_in[h, width:width + 1]
        )
        key_logit_grad = logit_grad(key_low, key_feat_grad)
        put_map(1, h, dot(k_ref[g], key_logit_grad, 0, 0))
        key_term = dot(key_logit_grad, w_ref[1, h], 1, 1)
        v_acc[g] += dot(key_low, back, 1, 1)
        fresh = h % group_size == 0

        @pl.when(fresh)
        def _():
            k_acc[...] = key_term

        @pl.when(jnp.logical_not(fresh))
        def _():
            k_acc[...] += key_term

        @pl.when(h % group_size == group_size - 1)
        def _():
            kg_ref[g] = k_acc[...].astype(BF16)
            vg_ref[g] = v_acc[g].astype(BF16)

        @pl.when(jnp.logical_and(h % batch == 1, h >= batch))
        def _():
            spread_map(1, h // batch - 1)

        return carry

    lax.fori_loop(0, heads, keys_side, 0)
    spread_map(1, batches - 1)

    for side in range(2):
        def finish(n, carry):
            total = map_sum[side, n, chip]
            for hop in range(1, chips):
                far_copy(side, n, hop).wait_recv()
                total += map_far[hop - 1, side, n]
            mg_ref[side, n] = total
            pair_copy(side, n).wait_send()
            for hop in range(1, chips):
                far_copy(side, n, hop).wait_send()
            return carry

        lax.fori_loop(0, batches, finish, 0)

    def drain(h, carry):
        @pl.when(me < blocks - 1)
        def _():
            fwd_copy(h).wait_send()

        @pl.when(me > 0)
        def _():
            bwd_copy(h).wait_send()

        return carry

    lax.fori_loop(0, heads, drain, 0)


def shards(chips, subs, queries, keys, values, out_grad, feature_weights):
    tokens, heads, width = queries.shape
    groups = keys.shape[1]
    feats = feature_weights.shape[3]
    rows = width // (chips * subs)
    batch = 4
    batches = heads // batch
    vmem = pl.BlockSpec(memory_space=pltpu.VMEM)
    slot = pltpu.VMEM((heads, width + 8, feats), F32)
    pieces = (2, batches, chips, batch, rows, feats)
    query_grad, key_grad, value_grad, maps = pl.pallas_call(
        functools.partial(kernel, chips, subs, heads // groups, batch),
        out_shape=(
            jax.ShapeDtypeStruct((heads, tokens, width), BF16),
            jax.ShapeDtypeStruct((groups, tokens, width), BF16),
            jax.ShapeDtypeStruct((groups, tokens, width), BF16),
            jax.ShapeDtypeStruct((2, batches, batch, rows, feats), F32),
        ),
        in_specs=[vmem] * 5,
        out_specs=(vmem,) * 4,
        scratch_shapes=[
            pltpu.VMEM((heads, tokens, feats), BF16),
            pltpu.VMEM((heads, tokens, feats), BF16),
            pltpu.VMEM((heads, tokens, feats), F32),
            slot, slot, slot, slot,
            pltpu.VMEM((tokens, width), F32),
            pltpu.VMEM((groups, tokens, width), F32),
            pltpu.VMEM((2, batches, subs, chips, batch, rows, feats), F32),
            pltpu.VMEM(pieces, F32),
            pltpu.VMEM(pieces, F32),
            pltpu.VMEM((chips - 1, 2, batches, batch, rows, feats), F32),
        ]
        + [pltpu.SemaphoreType.DMA((heads,))] * 4
        + [pltpu.SemaphoreType.DMA((2, batches))] * 2
        + [pltpu.SemaphoreType.DMA((chips - 1, 2, batches))] * 2,
        compiler_params=pltpu.CompilerParams(
            collective_id=0, has_side_effects=True, vmem_limit_bytes=58 * 1024 * 1024
        ),
    )(
        queries.transpose(1, 0, 2),
        keys.transpose(1, 0, 2),
        values.transpose(1, 0, 2),
        out_grad.transpose(1, 0, 2),
        feature_weights,
    )
    return (
        query_grad.transpose(1, 0, 2),
        key_grad.transpose(1, 0, 2),
        value_grad.transpose(1, 0, 2),
        maps.reshape(2, heads, rows, feats).transpose(2, 0, 1, 3),
    )


def solution(mesh):
    chips = mesh.shape["seq"]
    subs = mesh.shape["sub"]
    rows = P(("grp", "seq", "sub"), "head", None)
    return jax.shard_map(
        functools.partial(shards, chips, subs),
        mesh=mesh,
        in_specs=(rows, rows, rows, rows, P(None, "head", None, None)),
        out_specs=(rows, rows, rows, P(("grp", "seq", "sub"), None, "head", None)),
        check_vma=False,
    )
```
